1024 devices in a mesh: replica: 16 (over y_hi, z), fsdp: 32 (over x, y_lo), tensor: 2 (over core).
Axes of the slice: x: 8, y: 8 (y_hi: 2, y_lo: 4; y = y_hi * 4 + y_lo), z: 8, core: 2. Of those that a mesh axis runs over, the one named last changes fastest.
Arguments:
- pre_act: bfloat16 [4096, 24576], P('replica', ('fsdp', 'tensor')), may hold values from -6 to 6
- act_grad: bfloat16 [4096, 24576], P('replica', ('fsdp', 'tensor')), may hold values from -6 to 6
- up_weight: bfloat16 [6144, 24576], P('replica', ('fsdp', 'tensor')), may hold values from -0.0390625 to 0.0390625
- resid_grad: bfloat16 [4096, 6144], P('replica', ('fsdp', 'tensor')), may hold values from -3 to 3
- gram_parts: bfloat16 [16, 12288, 1024], P('replica', ('fsdp', 'tensor')), may hold values from -1.5 to 1.5
- stripe_order: int32 [64, 16], P(('fsdp', 'tensor')), may hold values from 0 to 15, each once within a row
- gram_prev: float32 [64, 16, 12, 1024], P(('fsdp', 'tensor'), 'replica'), may hold values from -6 to 6
Outputs:
- input_grad: bfloat16 [4096, 6144], P('replica', ('fsdp', 'tensor'))
- gram_stats: float32 [64, 16, 12, 1024], P(('fsdp', 'tensor'), 'replica')
The draws below stay inside these ranges and needn't reach their ends.
Inputs may be any that keep to these rules, and one draw needn't show every extreme that they name: Each row of stripe_order names every stripe 0 to 15 exactly once.
All inputs are finite; a program needn't handle non-finite values.
Results may differ from the reference program's by a relative error of at most 0.015.
Values may be sent and summed in bfloat16 or wider, within the bound.
No kernel may reach another device: no remote copies, remote signals or barrier semaphores. Data moves between devices by JAX's collectives and lax.ppermute only.
A program may use at most 32 MiB of HBM per device.

```python
import jax
import jax.numpy as jnp
from jax import lax

D = 6144
BLK = 1024
TOK_DEV = 256
HID = 24576
TOKENS = 4096
GRAM_ROWS = 12288
GROUPS = 64
STRIPE = 12
N_REPLICA = 16
N_FSDP = 32
N_TENSOR = 2


def block_scale(stream_key, extent, shards, smallest, high):
    loudness = 1.0
    for axis_at, blocks in shards:
        steps = jax.random.uniform(jax.random.fold_in(jax.random.fold_in(stream_key, 6), axis_at), (blocks,), jnp.float32, smallest / len(shards), high / len(shards))
        loudness = loudness * jnp.repeat(jnp.exp(steps), extent[axis_at] // blocks).reshape((-1,) + (1,) * (len(extent) - 1 - axis_at))
    return loudness


def gaussian(stream_key, dims, scale, reach, shards=(), held_as=jnp.bfloat16):
    entries = scale * jax.random.normal(stream_key, dims, jnp.float32)
    if shards:
        entries = entries * block_scale(stream_key, dims, shards, -0.22, 0.18)
    return jnp.clip(entries, -reach, reach).astype(held_as)


def setup_inputs(seed: int = 0) -> dict:
    key_list = jax.random.split(jax.random.key(seed), 8)
    return {
        "pre_act": gaussian(key_list[0], (TOKENS, HID), 1.0, 6.0, ((0, 16), (1, 64))),
        "act_grad": gaussian(key_list[1], (TOKENS, HID), 1.0, 6.0, ((0, 16), (1, 64))),
        "up_weight": gaussian(key_list[2], (D, HID), HID ** -0.5, 0.0390625, ((0, 16), (1, 64))),
        "resid_grad": gaussian(key_list[3], (TOKENS, D), 0.5, 3.0, ((0, 16), (1, 64))),
        "gram_parts": gaussian(key_list[4], (N_REPLICA, GRAM_ROWS, BLK), 0.25, 1.5, ((0, 16), (1, 64))),
        "stripe_order": jax.vmap(lambda own: jax.random.permutation(own, N_REPLICA))(jax.random.split(key_list[5], GROUPS)).reshape((GROUPS, N_REPLICA)).astype(jnp.int32),
        "gram_prev": gaussian(key_list[6], (GROUPS, N_REPLICA, STRIPE, BLK), 1.0, 6.0, ((0, 64), (1, 16)), jnp.float32),
    }


def gelu_slope(values):
    normal_cdf = 0.5 * (1.0 + jax.scipy.special.erf(values * 0.7071067811865476))
    return normal_cdf + values * jnp.exp(-0.5 * values * values) * 0.3989422804014327


def pick_stripes(stripes, ordering):
    return stripes[ordering]


def reference(pre_act, act_grad, up_weight, resid_grad, gram_parts, stripe_order, gram_prev):
    def backward(inputs):
        pre_block, grad_block, resid_block = inputs
        hidden_grad = (grad_block.astype(jnp.float32) * gelu_slope(pre_block.astype(jnp.float32))).astype(jnp.bfloat16)
        product = lax.dot_general(
            hidden_grad,
            up_weight,
            (((1,), (1,)), ((), ())),
            preferred_element_type=jnp.float32,
        )
        return (resid_block.astype(jnp.float32) + product).astype(jnp.bfloat16)

    blocks = (
        pre_act.reshape(N_REPLICA, TOK_DEV, HID),
        act_grad.reshape(N_REPLICA, TOK_DEV, HID),
        resid_grad.reshape(N_REPLICA, TOK_DEV, D),
    )
    input_grad = lax.map(backward, blocks).reshape(TOKENS, D)

    def accumulate(carry, slab):
        return carry + slab.astype(jnp.float32), None

    summed, _ = lax.scan(accumulate, jnp.zeros((GRAM_ROWS, BLK), jnp.float32), gram_parts)
    view = summed.reshape(N_FSDP * N_TENSOR, N_REPLICA, STRIPE, BLK)
    picked = jax.vmap(pick_stripes)(view, stripe_order)
    return input_grad, gram_prev + picked
```

```python
import jax
import jax.numpy as jnp
from jax import lax
from jax.sharding import Mesh, PartitionSpec as P


def gelu_slope(values):
    normal_cdf = 0.5 * (1.0 + jax.scipy.special.erf(values * 0.7071067811865476))
    return normal_cdf + values * jnp.exp(-0.5 * values * values) * 0.3989422804014327


SWAP = [(0, 1), (1, 0)]


def on_device(pre_act, act_grad, up_weight, resid_grad, gram_parts, stripe_order, gram_prev):
    core = lax.axis_index("core")
    y_hi = lax.axis_index("y_hi")
    tokens, hidden = pre_act.shape
    feats = resid_grad.shape[1]

    rows = up_weight.reshape(2, 2, feats, hidden)
    own = lax.dynamic_index_in_dim(rows, core, 1, keepdims=False)
    away = lax.dynamic_index_in_dim(rows, 1 - core, 1, keepdims=False)
    other = lax.ppermute(away, "core", SWAP)
    pair = jnp.concatenate([own, other], axis=-1).reshape(2 * feats, 2 * hidden)
    weight = lax.all_gather(pair, "z", axis=0, tiled=True)

    hidden_grad = (act_grad.astype(jnp.float32) * gelu_slope(pre_act.astype(jnp.float32))).astype(jnp.bfloat16)
    far = lax.ppermute(hidden_grad, "y_hi", SWAP)
    both = jnp.stack([jnp.where(y_hi == 0, hidden_grad, far), jnp.where(y_hi == 0, far, hidden_grad)])
    both = jnp.concatenate([both, lax.ppermute(both, "core", SWAP)], axis=-1)

    owners = lax.axis_size(("y_hi", "z"))
    stripes = gram_parts[0].reshape(owners, -1, gram_parts.shape[2])
    ordered = stripes[stripe_order[0]]
    kept = lax.all_to_all(ordered, ("y_hi", "z"), 0, 0, tiled=True)
    gram_stats = gram_prev + jnp.sum(kept.astype(jnp.float32), axis=0).reshape(gram_prev.shape)

    contract = (((1,), (1,)), ((), ()))
    partial = jnp.stack(
        [
            lax.dot_general(weight, both[i], contract, preferred_element_type=jnp.float32).astype(jnp.bfloat16)
            for i in range(2)
        ]
    )
    blocks = partial.reshape(-1, feats, tokens)
    arrived = lax.all_to_all(blocks, ("x_hi", "x_lo", "y_lo"), 0, 0, tiled=True)
    shared = jnp.sum(arrived.astype(jnp.float32), axis=0).astype(jnp.bfloat16)
    home = lax.ppermute(shared, ("y_hi", "x_hi"), [(0, 0), (1, 2), (2, 1), (3, 3)])
    input_grad = (home.astype(jnp.float32) + resid_grad.T.astype(jnp.float32)).astype(jnp.bfloat16).T
    return (input_grad, gram_stats)


def solution(mesh):
    fine = Mesh(mesh.devices.reshape(2, 8, 2, 4, 4, 2), ("y_hi", "z", "x_hi", "x_lo", "y_lo", "core"))
    replica = ("y_hi", "z")
    spread = ("x_hi", "x_lo", "y_lo", "core")
    return jax.shard_map(
        on_device,
        mesh=fine,
        in_specs=(
            P(replica, spread),
            P(replica, spread),
            P(replica, spread),
            P(replica, spread),
            P(replica, spread, None),
            P(spread, None),
            P(spread, replica, None, None),
        ),
        out_specs=(P(replica, spread), P(spread, replica, None, None)),
        check_vma=False,
    )
```

```python
import jax
import jax.numpy as jnp
from jax import lax
from jax.sharding import Mesh, PartitionSpec as P


def gelu_slope(values):
    normal_cdf = 0.5 * (1.0 + jax.scipy.special.erf(values * 0.7071067811865476))
    return normal_cdf + values * jnp.exp(-0.5 * values * values) * 0.3989422804014327


SWAP = [(0, 1), (1, 0)]
CHUNKS = ((0, 40), (40, 96))


def on_device(pre_act, act_grad, up_weight, resid_grad, gram_parts, stripe_order, gram_prev):
    core = lax.axis_index("core")
    y_hi = lax.axis_index("y_hi")
    tokens, hidden = pre_act.shape
    feats = resid_grad.shape[1]

    rows = up_weight.reshape(2, 2, feats, hidden)
    own = lax.dynamic_index_in_dim(rows, core, 1, keepdims=False)
    away = lax.dynamic_index_in_dim(rows, 1 - core, 1, keepdims=False)
    other = lax.ppermute(away, "core", SWAP)
    pair = jnp.concatenate([own, other], axis=-1)
    weights = [
        lax.all_gather(pair[:, lo:hi].reshape(-1, 2 * hidden), "z", axis=0, tiled=True) for lo, hi in CHUNKS
    ]

    hidden_grad = (act_grad.astype(jnp.float32) * gelu_slope(pre_act.astype(jnp.float32))).astype(jnp.bfloat16)
    far = lax.ppermute(hidden_grad, "y_hi", SWAP)
    both = jnp.stack([jnp.where(y_hi == 0, hidden_grad, far), jnp.where(y_hi == 0, far, hidden_grad)])
    both = jnp.concatenate([both, lax.ppermute(both, "core", SWAP)], axis=-1)

    owners = lax.axis_size(("y_hi", "z"))
    stripes = gram_parts[0].reshape(owners, -1, gram_parts.shape[2])
    ordered = stripes[stripe_order[0]]
    kept = lax.all_to_all(ordered, ("y_hi", "z"), 0, 0, tiled=True)
    gram_stats = gram_prev + jnp.sum(kept.astype(jnp.float32), axis=0).reshape(gram_prev.shape)

    contract = (((1,), (1,)), ((), ()))
    homes = []
    for (lo, hi), weight in zip(CHUNKS, weights):
        partial = jnp.stack(
            [
                lax.dot_general(weight, both[i], contract, preferred_element_type=jnp.float32).astype(jnp.bfloat16)
                for i in range(2)
            ]
        )
        blocks = partial.reshape(-1, hi - lo, tokens)
        arrived = lax.all_to_all(blocks, ("x_hi", "x_lo", "y_lo"), 0, 0, tiled=True)
        shared = jnp.sum(arrived.astype(jnp.float32), axis=0).astype(jnp.bfloat16)
        homes.append(lax.ppermute(shared, ("y_hi", "x_hi"), [(0, 0), (1, 2), (2, 1), (3, 3)]))
    home = jnp.concatenate(homes, axis=0)
    input_grad = (home.astype(jnp.float32) + resid_grad.T.astype(jnp.float32)).astype(jnp.bfloat16).T
    return (input_grad, gram_stats)


def solution(mesh):
    fine = Mesh(mesh.devices.reshape(2, 8, 2, 4, 4, 2), ("y_hi", "z", "x_hi", "x_lo", "y_lo", "core"))
    replica = ("y_hi", "z")
    spread = ("x_hi", "x_lo", "y_lo", "core")
    return jax.shard_map(
        on_device,
        mesh=fine,
        in_specs=(
            P(replica, spread),
            P(replica, spread),
            P(replica, spread),
            P(replica, spread),
            P(replica, spread, None),
            P(spread, None),
            P(spread, replica, None, None),
        ),
        out_specs=(P(replica, spread), P(spread, replica, None, None)),
        check_vma=False,
    )
```

```python
import jax
import jax.numpy as jnp
from jax import lax
from jax.sharding import Mesh, PartitionSpec as P


def gelu_slope(values):
    normal_cdf = 0.5 * (1.0 + jax.scipy.special.erf(values * 0.7071067811865476))
    return normal_cdf + values * jnp.exp(-0.5 * values * values) * 0.3989422804014327


SWAP = [(0, 1), (1, 0)]
QUAD = ("x_lo", "core")


def last_hop(flip):
    pairs = []
    for y in range(2):
        for q in range(4):
            for b in range(2):
                pairs.append((y * 8 + q * 2 + b, (b ^ flip) * 8 + y * 4 + q))
    return pairs


def on_device(pre_act, act_grad, up_weight, resid_grad, gram_parts, stripe_order, gram_prev):
    core = lax.axis_index("core")
    x_lo = lax.axis_index("x_lo")
    y_hi = lax.axis_index("y_hi")
    tokens, hidden = pre_act.shape
    half = resid_grad.shape[1] // 2

    rows = up_weight.reshape(2, 2, 2, half, hidden)

    def quarter(x_flip, core_flip):
        piece = lax.dynamic_slice(rows, (0, core ^ core_flip, x_lo ^ x_flip, 0, 0), (2, 1, 1, half, hidden))
        piece = piece.reshape(2 * half, hidden)
        if x_flip or core_flip:
            step = 2 * x_flip + core_flip
            piece = lax.ppermute(piece, QUAD, [(i, i ^ step) for i in range(4)])
        return piece

    pair = jnp.concatenate([quarter(0, 0), quarter(1, 0), quarter(0, 1), quarter(1, 1)], axis=-1)
    weight = lax.all_gather(pair, "z", axis=0, tiled=True)

    hidden_grad = (act_grad.astype(jnp.float32) * gelu_slope(pre_act.astype(jnp.float32))).astype(jnp.bfloat16)
    far = lax.ppermute(hidden_grad, "y_hi", SWAP)
    both = jnp.concatenate([hidden_grad, far], axis=0)
    both = jnp.stack([both, lax.ppermute(both, "x_lo", SWAP)])
    mate = lax.ppermute(both, "core", SWAP)
    both = jnp.concatenate([both[0], both[1], mate[0], mate[1]], axis=-1)

    owners = lax.axis_size(("y_hi", "z"))
    stripes = gram_parts[0].reshape(owners, -1, gram_parts.shape[2])
    ordered = stripes[stripe_order[0]]
    kept = lax.all_to_all(ordered, ("y_hi", "z"), 0, 0, tiled=True)
    gram_stats = gram_prev + jnp.sum(kept.astype(jnp.float32), axis=0).reshape(gram_prev.shape)

    partial = lax.dot_general(
        weight, both, (((1,), (1,)), ((), ())), preferred_element_type=jnp.float32
    ).astype(jnp.bfloat16)
    blocks = partial.reshape(-1, half, 2 * tokens)
    arrived = lax.all_to_all(blocks, ("x_hi", "x_mid", "y_lo"), 0, 0, tiled=True)
    shared = jnp.sum(arrived.astype(jnp.float32), axis=0).astype(jnp.bfloat16)
    own, away = shared[:, :tokens], shared[:, tokens:]
    where = ("y_hi", "x_hi", "x_mid", "x_lo")
    one = lax.ppermute(jnp.where(x_lo == y_hi, own, away), where, last_hop(0))
    two = lax.ppermute(jnp.where(x_lo == y_hi, away, own), where, last_hop(1))
    home = jnp.concatenate([jnp.where(y_hi == 0, one, two), jnp.where(y_hi == 0, two, one)], axis=0)
    input_grad = (home.astype(jnp.float32) + resid_grad.T.astype(jnp.float32)).astype(jnp.bfloat16).T
    return (input_grad, gram_stats)


def solution(mesh):
    axes = ("y_hi", "z", "x_hi", "x_mid", "x_lo", "y_lo", "core")
    fine = Mesh(mesh.devices.reshape(2, 8, 2, 2, 2, 4, 2), axes)
    replica, spread = axes[:2], axes[2:]
    return jax.shard_map(
        on_device,
        mesh=fine,
        in_specs=(
            P(replica, spread),
            P(replica, spread),
            P(replica, spread),
            P(replica, spread),
            P(replica, spread, None),
            P(spread, None),
            P(spread, replica, None, None),
        ),
        out_specs=(P(replica, spread), P(spread, replica, None, None)),
        check_vma=False,
    )
```

```python
import jax
import jax.numpy as jnp
from jax import lax
from jax.sharding import Mesh, PartitionSpec as P


def gelu_slope(values):
    normal_cdf = 0.5 * (1.0 + jax.scipy.special.erf(values * 0.7071067811865476))
    return normal_cdf + values * jnp.exp(-0.5 * values * values) * 0.3989422804014327


SWAP = [(0, 1), (1, 0)]
QUAD = ("x_lo", "core")
WHERE = ("y_hi", "x_hi", "x_mid", "x_lo", "y_lo")


def last_hop():
    pairs = []
    for y in range(2):
        for x in range(8):
            for low in range(4):
                s, z2, b, z1, z0 = x >> 2, (x >> 1) & 1, x & 1, low >> 1, low & 1
                pairs.append(((y * 8 + x) * 4 + low, ((y ^ s) * 8 + y * 4 + z2 * 2 + z1) * 4 + z0 * 2 + b))
    return pairs


def beside(parts):
    return jnp.concatenate([parts[i] for i in range(parts.shape[0])], axis=-1)


def on_device(pre_act, act_grad, up_weight, resid_grad, gram_parts, stripe_order, gram_prev):
    tokens, hidden = pre_act.shape
    feats = resid_grad.shape[1]

    quarters = lax.all_to_all(up_weight.reshape(4, feats, hidden), QUAD, 0, 0, tiled=True)
    weight = lax.all_gather(beside(quarters), "z", axis=0, tiled=True)

    hidden_grad = (act_grad.astype(jnp.float32) * gelu_slope(pre_act.astype(jnp.float32))).astype(jnp.bfloat16)
    far_grad = lax.ppermute(hidden_grad, "y_hi", SWAP)
    own = beside(lax.all_gather(hidden_grad, QUAD, axis=0))
    far = beside(lax.all_gather(far_grad, QUAD, axis=0))

    owners = lax.axis_size(("y_hi", "z"))
    stripes = gram_parts[0].reshape(owners, -1, gram_parts.shape[2])
    ordered = stripes[stripe_order[0]]
    kept = lax.all_to_all(ordered, ("y_hi", "z"), 0, 0, tiled=True)
    weight, kept = lax.optimization_barrier((weight, kept))
    gram_stats = gram_prev + jnp.sum(kept.astype(jnp.float32), axis=0).reshape(gram_prev.shape)

    contract = (((1,), (1,)), ((), ()))
    partial = jnp.stack(
        [
            lax.dot_general(weight, grads, contract, preferred_element_type=jnp.float32).astype(jnp.bfloat16)
            for grads in (own, far)
        ]
    )
    blocks = partial.reshape(-1, feats, tokens)
    arrived = lax.all_to_all(blocks, ("x_hi", "x_mid", "y_lo"), 0, 0, tiled=True)
    shared = jnp.sum(arrived.astype(jnp.float32), axis=0).astype(jnp.bfloat16)
    home = lax.ppermute(shared, WHERE, last_hop())
    input_grad = (home.astype(jnp.float32) + resid_grad.T.astype(jnp.float32)).astype(jnp.bfloat16).T
    return (input_grad, gram_stats)


def solution(mesh):
    axes = ("y_hi", "z", "x_hi", "x_mid", "x_lo", "y_lo", "core")
    fine = Mesh(mesh.devices.reshape(2, 8, 2, 2, 2, 4, 2), axes)
    replica, spread = axes[:2], axes[2:]
    return jax.shard_map(
        on_device,
        mesh=fine,
        in_specs=(
            P(replica, spread),
            P(replica, spread),
            P(replica, spread),
            P(replica, spread),
            P(replica, spread, None),
            P(spread, None),
            P(spread, replica, None, None),
        ),
        out_specs=(P(replica, spread), P(spread, replica, None, None)),
        check_vma=False,
    )
```

```python
import jax
import jax.numpy as jnp
from jax import lax
from jax.sharding import Mesh, PartitionSpec as P


def gelu_slope(values):
    normal_cdf = 0.5 * (1.0 + jax.scipy.special.erf(values * 0.7071067811865476))
    return normal_cdf + values * jnp.exp(-0.5 * values * values) * 0.3989422804014327


SWAP = [(0, 1), (1, 0)]
QUAD = ("x_lo", "core")
WHERE = ("y_hi", "z", "x_hi", "x_mid", "x_lo", "y_lo")
ORDER = (0, 1, 7, 2, 6, 3, 5, 4)


def from_z(value, step):
    return lax.ppermute(value, "z", [((i + step) % 8, i) for i in range(8)])


def last_hop():
    pairs = []
    for y in range(2):
        for z in range(8):
            for x in range(8):
                for low in range(4):
                    s, b, p = x >> 2, x & 1, ((x >> 1) & 1) * 4 + low
                    w = (z + ORDER[p]) % 8
                    target = (((y ^ s) * 8 + z) * 8 + y * 4 + (w >> 1)) * 4 + (w & 1) * 2 + b
                    pairs.append((((y * 8 + z) * 8 + x) * 4 + low, target))
    return pairs


def beside(parts):
    return jnp.concatenate([parts[i] for i in range(parts.shape[0])], axis=-1)


def on_device(pre_act, act_grad, up_weight, resid_grad, gram_parts, stripe_order, gram_prev):
    tokens, hidden = pre_act.shape
    feats = resid_grad.shape[1]

    hidden_grad = (act_grad.astype(jnp.float32) * gelu_slope(pre_act.astype(jnp.float32))).astype(jnp.bfloat16)
    far_grad = lax.ppermute(hidden_grad, "y_hi", SWAP)

    owners = lax.axis_size(("y_hi", "z"))
    stripes = gram_parts[0].reshape(owners, -1, gram_parts.shape[2])
    ordered = stripes[stripe_order[0]]

    quarters = lax.all_to_all(up_weight.reshape(4, feats, hidden), QUAD, 0, 0, tiled=True)
    mine = beside(quarters)
    mine, hidden_grad, ordered = lax.optimization_barrier((mine, hidden_grad, ordered))
    ring = {0: mine}
    for step in (2, 6, 1, 7):
        ring[step] = from_z(mine, step)
    ring[3] = from_z(ring[2], 1)
    ring[5] = from_z(ring[6], 7)
    mid = feats // 2
    ring[4] = jnp.concatenate([from_z(ring[2][:mid], 2), from_z(ring[6][mid:], 6)], axis=0)

    own = beside(lax.all_gather(hidden_grad, QUAD, axis=0))
    far_grad, own = lax.optimization_barrier((far_grad, own))
    far = beside(lax.all_gather(far_grad, QUAD, axis=0))
    kept = lax.all_to_all(ordered, ("y_hi", "z"), 0, 0, tiled=True)
    ring[4], kept = lax.optimization_barrier((ring[4], kept))
    gram_stats = gram_prev + jnp.sum(kept.astype(jnp.float32), axis=0).reshape(gram_prev.shape)

    contract = (((1,), (1,)), ((), ()))
    pieces = []
    for grads in (own, far):
        for group in (ORDER[:5], ORDER[5:]):
            weight = jnp.concatenate([ring[step] for step in group], axis=0)
            product = lax.dot_general(weight, grads, contract, preferred_element_type=jnp.float32)
            pieces.append(product.astype(jnp.bfloat16))
    blocks = jnp.concatenate(pieces, axis=0).reshape(-1, feats, tokens)
    arrived = lax.all_to_all(blocks, ("x_hi", "x_mid", "y_lo"), 0, 0, tiled=True)
    shared = jnp.sum(arrived.astype(jnp.float32), axis=0).astype(jnp.bfloat16)
    home = lax.ppermute(shared, WHERE, last_hop())
    input_grad = (home.astype(jnp.float32) + resid_grad.T.astype(jnp.float32)).astype(jnp.bfloat16).T
    return (input_grad, gram_stats)


def solution(mesh):
    axes = ("y_hi", "z", "x_hi", "x_mid", "x_lo", "y_lo", "core")
    fine = Mesh(mesh.devices.reshape(2, 8, 2, 2, 2, 4, 2), axes)
    replica, spread = axes[:2], axes[2:]
    return jax.shard_map(
        on_device,
        mesh=fine,
        in_specs=(
            P(replica, spread),
            P(replica, spread),
            P(replica, spread),
            P(replica, spread),
            P(replica, spread, None),
            P(spread, None),
            P(spread, replica, None, None),
        ),
        out_specs=(P(replica, spread), P(spread, replica, None, None)),
        check_vma=False,
    )
```

```python
import jax
import jax.numpy as jnp
from jax import lax
from jax.experimental import pallas as pl
from jax.experimental.pallas import tpu as pltpu
from jax.sharding import Mesh, PartitionSpec as P


def gelu_slope(values):
    normal_cdf = 0.5 * (1.0 + jax.scipy.special.erf(values * 0.7071067811865476))
    return normal_cdf + values * jnp.exp(-0.5 * values * values) * 0.3989422804014327


SWAP = [(0, 1), (1, 0)]
QUAD = ("x_lo", "core")
WHERE = ("y_hi", "z", "x_hi", "x_mid", "x_lo", "y_lo")
ORDER = (0, 1, 7, 2, 6, 3, 5, 4)


def from_z(value, step):
    return lax.ppermute(value, "z", [((i + step) % 8, i) for i in range(8)])


def last_hop():
    pairs = []
    for y in range(2):
        for z in range(8):
            for x in range(8):
                for low in range(4):
                    s, b, p = x >> 2, x & 1, ((x >> 1) & 1) * 4 + low
                    w = (z + ORDER[p]) % 8
                    target = (((y ^ s) * 8 + z) * 8 + y * 4 + (w >> 1)) * 4 + (w & 1) * 2 + b
                    pairs.append((((y * 8 + z) * 8 + x) * 4 + low, target))
    return pairs


def beside(parts):
    return jnp.concatenate([parts[i] for i in range(parts.shape[0])], axis=-1)


def products(own, far, pieces, feats, before=None):
    sources, tokens, hidden = own.shape
    rows = sum(piece.shape[0] for piece in pieces)
    done = 0 if before is None else before.shape[1]

    def kernel(*refs):
        own_ref, far_ref, out_ref = refs[0], refs[1], refs[-1]
        piece_refs = refs[2 : 2 + len(pieces)]
        for slot, grads_ref in enumerate((own_ref, far_ref)):
            total = None
            for source in range(sources):
                columns = slice(source * hidden, (source + 1) * hidden)
                weight = jnp.concatenate([ref[:, columns] for ref in piece_refs], axis=0)
                term = lax.dot_general(
                    weight, grads_ref[source], (((1,), (1,)), ((), ())), preferred_element_type=jnp.float32
                )
                total = term if total is None else total + term
            if before is not None:
                out_ref[slot, :done] = refs[2 + len(pieces)][slot]
            out_ref[slot, done:] = total.astype(jnp.bfloat16)

    operands = [own, far, *pieces] + ([] if before is None else [before])
    return pl.pallas_call(
        kernel,
        out_shape=jax.ShapeDtypeStruct((2, done + rows, tokens), jnp.bfloat16),
        in_specs=[pl.BlockSpec(memory_space=pltpu.VMEM)] * len(operands),
        out_specs=pl.BlockSpec(memory_space=pltpu.VMEM),
        compiler_params=pltpu.CompilerParams(vmem_limit_bytes=32 * 1024 * 1024),
        cost_estimate=pl.CostEstimate(
            flops=4 * rows * tokens * sources * hidden, bytes_accessed=6000000, transcendentals=0
        ),
    )(*operands)


def on_device(pre_act, act_grad, up_weight, resid_grad, gram_parts, stripe_order, gram_prev):
    tokens, hidden = pre_act.shape
    feats = resid_grad.shape[1]

    hidden_grad = (act_grad.astype(jnp.float32) * gelu_slope(pre_act.astype(jnp.float32))).astype(jnp.bfloat16)
    far_grad = lax.ppermute(hidden_grad, "y_hi", SWAP)

    quarters = lax.all_to_all(up_weight.reshape(4, feats, hidden), QUAD, 0, 0, tiled=True)
    mine = beside(quarters)
    mine, hidden_grad = lax.optimization_barrier((mine, hidden_grad))
    ring = {0: mine}
    for step in (2, 6, 1, 7):
        ring[step] = from_z(mine, step)
    own = lax.all_gather(hidden_grad, QUAD, axis=0)
    own, parts = lax.optimization_barrier((own, gram_parts[0]))
    stripes = parts.reshape(lax.axis_size(("y_hi", "z")), -1, parts.shape[1])
    ordered = stripes[stripe_order[0]]

    *first, far_grad, own, ordered = lax.optimization_barrier(
        (ring[1], ring[7], ring[2], ring[6], far_grad, own, ordered)
    )
    ring[1], ring[7], ring[2], ring[6] = first
    ring[3] = from_z(ring[2], 1)
    ring[5] = from_z(ring[6], 7)
    mid = feats // 2
    upper, lower = from_z(ring[2][:mid], 2), from_z(ring[6][mid:], 6)
    far = lax.all_gather(far_grad, QUAD, axis=0)
    kept = lax.all_to_all(ordered, ("y_hi", "z"), 0, 0, tiled=True)

    near = products(own, far, [ring[step] for step in ORDER[:5]], feats)
    upper, kept = lax.optimization_barrier((upper, kept))
    gram_stats = gram_prev + jnp.sum(kept.astype(jnp.float32), axis=0).reshape(gram_prev.shape)
    blocks = products(own, far, [ring[3], ring[5], upper, lower], feats, near)
    blocks = blocks.reshape(-1, feats, tokens)
    arrived = lax.all_to_all(blocks, ("x_hi", "x_mid", "y_lo"), 0, 0, tiled=True)
    shared = jnp.sum(arrived.astype(jnp.float32), axis=0).astype(jnp.bfloat16)
    home = lax.ppermute(shared, WHERE, last_hop())
    input_grad = (home.astype(jnp.float32) + resid_grad.T.astype(jnp.float32)).astype(jnp.bfloat16).T
    return (input_grad, gram_stats)


def solution(mesh):
    axes = ("y_hi", "z", "x_hi", "x_mid", "x_lo", "y_lo", "core")
    fine = Mesh(mesh.devices.reshape(2, 8, 2, 2, 2, 4, 2), axes)
    replica, spread = axes[:2], axes[2:]
    return jax.shard_map(
        on_device,
        mesh=fine,
        in_specs=(
            P(replica, spread),
            P(replica, spread),
            P(replica, spread),
            P(replica, spread),
            P(replica, spread, None),
            P(spread, None),
            P(spread, replica, None, None),
        ),
        out_specs=(P(replica, spread), P(spread, replica, None, None)),
        check_vma=False,
    )
```

```python
import jax
import jax.numpy as jnp
from jax import lax
from jax.experimental import pallas as pl
from jax.experimental.pallas import tpu as pltpu
from jax.sharding import Mesh, PartitionSpec as P


def gelu_slope(values):
    normal_cdf = 0.5 * (1.0 + jax.scipy.special.erf(values * 0.7071067811865476))
    return normal_cdf + values * jnp.exp(-0.5 * values * values) * 0.3989422804014327


SWAP = [(0, 1), (1, 0)]
QUAD = ("x_lo", "core")
WHERE = ("y_hi", "z", "x_hi", "x_mid", "x_lo", "y_lo")
ORDER = (0, 1, 7, 2, 6, 3, 5, 4)


def from_z(value, step):
    return lax.ppermute(value, "z", [((i + step) % 8, i) for i in range(8)])


def last_hop():
    pairs = []
    for y in range(2):
        for z in range(8):
            for x in range(8):
                for low in range(4):
                    s, b, p = x >> 2, x & 1, ((x >> 1) & 1) * 4 + low
                    w = (z + ORDER[p]) % 8
                    target = (((y ^ s) * 8 + z) * 8 + y * 4 + (w >> 1)) * 4 + (w & 1) * 2 + b
                    pairs.append((((y * 8 + z) * 8 + x) * 4 + low, target))
    return pairs


def beside(parts):
    return jnp.concatenate([parts[i] for i in range(parts.shape[0])], axis=-1)


def products(own, far, pieces, x_lo):
    cores, places, tokens, hidden = own.shape
    rows = sum(piece.shape[0] for piece in pieces)

    def kernel(x_ref, own_ref, far_ref, *refs):
        piece_refs, out_ref = refs[:-1], refs[-1]
        here = x_ref[0]
        for slot, grads_ref in enumerate((own_ref, far_ref)):
            total = None
            for place in range(places):
                at = here if place == 0 else 1 - here
                for core in range(cores):
                    source = place * cores + core
                    columns = slice(source * hidden, (source + 1) * hidden)
                    weight = jnp.concatenate([ref[:, columns] for ref in piece_refs], axis=0)
                    term = lax.dot_general(
                        weight, grads_ref[core, at], (((1,), (1,)), ((), ())), preferred_element_type=jnp.float32
                    )
                    total = term if total is None else total + term
            out_ref[slot] = total.astype(jnp.bfloat16)

    in_vmem = pl.BlockSpec(memory_space=pltpu.VMEM)
    return pl.pallas_call(
        kernel,
        out_shape=jax.ShapeDtypeStruct((2, rows, tokens), jnp.bfloat16),
        in_specs=[pl.BlockSpec(memory_space=pltpu.SMEM)] + [in_vmem] * (2 + len(pieces)),
        out_specs=in_vmem,
        compiler_params=pltpu.CompilerParams(vmem_limit_bytes=32 * 1024 * 1024),
        cost_estimate=pl.CostEstimate(
            flops=4 * rows * tokens * cores * places * hidden, bytes_accessed=6000000, transcendentals=0
        ),
    )(x_lo.reshape(1).astype(jnp.int32), own, far, *pieces)


def on_device(pre_act, act_grad, up_weight, resid_grad, gram_parts, stripe_order, gram_prev):
    tokens, hidden = pre_act.shape
    feats = resid_grad.shape[1]

    hidden_grad = (act_grad.astype(jnp.float32) * gelu_slope(pre_act.astype(jnp.float32))).astype(jnp.bfloat16)
    far_grad = lax.ppermute(hidden_grad, "y_hi", SWAP)
    beside_grad = lax.ppermute(hidden_grad, "x_lo", SWAP)

    quarters = lax.all_to_all(up_weight.reshape(4, feats, hidden), QUAD, 0, 0, tiled=True)
    mine = beside(quarters)
    mine, hidden_grad = lax.optimization_barrier((mine, hidden_grad))
    ring = {0: mine}
    for step in (2, 6, 1, 7):
        ring[step] = from_z(mine, step)
    own = lax.all_gather(jnp.stack([hidden_grad, beside_grad]), "core", axis=0)
    own, parts, far_grad = lax.optimization_barrier((own, gram_parts[0], far_grad))
    far_pair = jnp.stack([far_grad, lax.ppermute(far_grad, "x_lo", SWAP)])
    stripes = parts.reshape(lax.axis_size(("y_hi", "z")), -1, parts.shape[1])
    ordered = stripes[stripe_order[0]]

    *first, far_pair, own, ordered = lax.optimization_barrier(
        (ring[1], ring[7], ring[2], ring[6], far_pair, own, ordered)
    )
    ring[1], ring[7], ring[2], ring[6] = first
    ring[3] = from_z(ring[2], 1)
    ring[5] = from_z(ring[6], 7)
    mid = feats // 2
    upper, lower = from_z(ring[2][:mid], 2), from_z(ring[6][mid:], 6)
    far = lax.all_gather(far_pair, "core", axis=0)

    kept = lax.all_to_all(ordered, ("y_hi", "z"), 0, 0, tiled=True)
    upper, kept = lax.optimization_barrier((upper, kept))
    gram_stats = gram_prev + jnp.sum(kept.astype(jnp.float32), axis=0).reshape(gram_prev.shape)

    pieces = [ring[step] for step in ORDER[:-1]] + [upper, lower]
    blocks = products(own, far, pieces, lax.axis_index("x_lo")).reshape(-1, feats, tokens)
    arrived = lax.all_to_all(blocks, ("x_hi", "x_mid", "y_lo"), 0, 0, tiled=True)
    shared = jnp.sum(arrived.astype(jnp.float32), axis=0).astype(jnp.bfloat16)
    home = lax.ppermute(shared, WHERE, last_hop())
    input_grad = (home.astype(jnp.float32) + resid_grad.T.astype(jnp.float32)).astype(jnp.bfloat16).T
    return (input_grad, gram_stats)


def solution(mesh):
    axes = ("y_hi", "z", "x_hi", "x_mid", "x_lo", "y_lo", "core")
    fine = Mesh(mesh.devices.reshape(2, 8, 2, 2, 2, 4, 2), axes)
    replica, spread = axes[:2], axes[2:]
    return jax.shard_map(
        on_device,
        mesh=fine,
        in_specs=(
            P(replica, spread),
            P(replica, spread),
            P(replica, spread),
            P(replica, spread),
            P(replica, spread, None),
            P(spread, None),
            P(spread, replica, None, None),
        ),
        out_specs=(P(replica, spread), P(spread, replica, None, None)),
        check_vma=False,
    )
```

```python
import jax
import jax.numpy as jnp
from jax import lax
from jax.experimental import pallas as pl
from jax.experimental.pallas import tpu as pltpu
from jax.sharding import Mesh, PartitionSpec as P


def gelu_slope(values):
    normal_cdf = 0.5 * (1.0 + jax.scipy.special.erf(values * 0.7071067811865476))
    return normal_cdf + values * jnp.exp(-0.5 * values * values) * 0.3989422804014327


SWAP = [(0, 1), (1, 0)]
QUAD = ("x_lo", "core")
WHERE = ("y_hi", "z", "x_hi", "x_mid", "x_lo", "y_lo")
ORDER = (0, 1, 7, 2, 6, 3, 5, 4)


def from_z(value, step):
    return lax.ppermute(value, "z", [((i + step) % 8, i) for i in range(8)])


def last_hop():
    pairs = []
    for y in range(2):
        for z in range(8):
            for x in range(8):
                for low in range(4):
                    s, b, p = x >> 2, x & 1, ((x >> 1) & 1) * 4 + low
                    w = (z + ORDER[p]) % 8
                    target = (((y ^ s) * 8 + z) * 8 + y * 4 + (w >> 1)) * 4 + (w & 1) * 2 + b
                    pairs.append((((y * 8 + z) * 8 + x) * 4 + low, target))
    return pairs


def beside(parts):
    return jnp.concatenate([parts[i] for i in range(parts.shape[0])], axis=-1)


def products(own, far, pieces, x_lo):
    cores, places, tokens, hidden = own.shape
    rows = sum(piece.shape[0] for piece in pieces)

    def kernel(x_ref, own_ref, far_ref, *refs):
        piece_refs, out_ref = refs[:-1], refs[-1]
        here = x_ref[0]
        for slot, grads_ref in enumerate((own_ref, far_ref)):
            total = None
            for place in range(places):
                at = here if place == 0 else 1 - here
                for core in range(cores):
                    source = place * cores + core
                    columns = slice(source * hidden, (source + 1) * hidden)
                    weight = jnp.concatenate([ref[:, columns] for ref in piece_refs], axis=0)
                    term = lax.dot_general(
                        weight, grads_ref[core, at], (((1,), (1,)), ((), ())), preferred_element_type=jnp.float32
                    )
                    total = term if total is None else total + term
            out_ref[slot] = total.astype(jnp.bfloat16)

    in_vmem = pl.BlockSpec(memory_space=pltpu.VMEM)
    return pl.pallas_call(
        kernel,
        out_shape=jax.ShapeDtypeStruct((2, rows, tokens), jnp.bfloat16),
        in_specs=[pl.BlockSpec(memory_space=pltpu.SMEM)] + [in_vmem] * (2 + len(pieces)),
        out_specs=in_vmem,
        compiler_params=pltpu.CompilerParams(vmem_limit_bytes=32 * 1024 * 1024),
        cost_estimate=pl.CostEstimate(
            flops=4 * rows * tokens * cores * places * hidden, bytes_accessed=6000000, transcendentals=0
        ),
    )(x_lo.reshape(1).astype(jnp.int32), own, far, *pieces)


def on_device(pre_act, act_grad, up_weight, resid_grad, gram_parts, stripe_order, gram_prev):
    tokens, hidden = pre_act.shape
    feats = resid_grad.shape[1]

    hidden_grad = (act_grad.astype(jnp.float32) * gelu_slope(pre_act.astype(jnp.float32))).astype(jnp.bfloat16)
    far_grad = lax.ppermute(hidden_grad, "y_hi", SWAP)
    beside_grad = lax.ppermute(hidden_grad, "x_lo", SWAP)

    quarters = lax.all_to_all(up_weight.reshape(4, feats, hidden), QUAD, 0, 0, tiled=True)
    mine = beside(quarters)
    mine, hidden_grad = lax.optimization_barrier((mine, hidden_grad))
    ring = {0: mine}
    for step in (2, 6, 1, 7, 4):
        ring[step] = from_z(mine, step)
    own = lax.all_gather(jnp.stack([hidden_grad, beside_grad]), "core", axis=0)
    own, parts, far_grad = lax.optimization_barrier((own, gram_parts[0], far_grad))
    far_pair = jnp.stack([far_grad, lax.ppermute(far_grad, "x_lo", SWAP)])
    stripes = parts.reshape(lax.axis_size(("y_hi", "z")), -1, parts.shape[1])
    ordered = stripes[stripe_order[0]]

    *first, far_pair, own, ordered = lax.optimization_barrier(
        (ring[1], ring[7], ring[2], ring[6], far_pair, own, ordered)
    )
    ring[1], ring[7], ring[2], ring[6] = first
    ring[3] = from_z(ring[2], 1)
    ring[5] = from_z(ring[6], 7)
    far = lax.all_gather(far_pair, "core", axis=0)

    kept = lax.all_to_all(ordered, ("y_hi", "z"), 0, 0, tiled=True)
    ring[3], kept = lax.optimization_barrier((ring[3], kept))
    gram_stats = gram_prev + jnp.sum(kept.astype(jnp.float32), axis=0).reshape(gram_prev.shape)

    blocks = products(own, far, [ring[step] for step in ORDER], lax.axis_index("x_lo")).reshape(-1, feats, tokens)
    arrived = lax.all_to_all(blocks, ("x_hi", "x_mid", "y_lo"), 0, 0, tiled=True)
    shared = jnp.sum(arrived.astype(jnp.float32), axis=0).astype(jnp.bfloat16)
    home = lax.ppermute(shared, WHERE, last_hop())
    input_grad = (home.astype(jnp.float32) + resid_grad.T.astype(jnp.float32)).astype(jnp.bfloat16).T
    return (input_grad, gram_stats)


def solution(mesh):
    axes = ("y_hi", "z", "x_hi", "x_mid", "x_lo", "y_lo", "core")
    fine = Mesh(mesh.devices.reshape(2, 8, 2, 2, 2, 4, 2), axes)
    replica, spread = axes[:2], axes[2:]
    return jax.shard_map(
        on_device,
        mesh=fine,
        in_specs=(
            P(replica, spread),
            P(replica, spread),
            P(replica, spread),
            P(replica, spread),
            P(replica, spread, None),
            P(spread, None),
            P(spread, replica, None, None),
        ),
        out_specs=(P(replica, spread), P(spread, replica, None, None)),
        check_vma=False,
    )
```

```python
import jax
import jax.numpy as jnp
from jax import lax
from jax.experimental import pallas as pl
from jax.experimental.pallas import tpu as pltpu
from jax.sharding import Mesh, PartitionSpec as P


def gelu_slope(values):
    normal_cdf = 0.5 * (1.0 + jax.scipy.special.erf(values * 0.7071067811865476))
    return normal_cdf + values * jnp.exp(-0.5 * values * values) * 0.3989422804014327


SWAP = [(0, 1), (1, 0)]
QUAD = ("x_lo", "core")
WHERE = ("y_hi", "z", "x_hi", "x_mid", "x_lo", "y_lo")
ORDER = (0, 1, 7, 2, 6, 3, 5, 4)


def from_z(value, step):
    return lax.ppermute(value, "z", [((i + step) % 8, i) for i in range(8)])


def last_hop():
    pairs = []
    for y in range(2):
        for z in range(8):
            for x in range(8):
                for low in range(4):
                    s, b, p = x >> 2, x & 1, ((x >> 1) & 1) * 4 + low
                    w = (z + ORDER[p]) % 8
                    target = (((y ^ s) * 8 + z) * 8 + y * 4 + (w >> 1)) * 4 + (w & 1) * 2 + b
                    pairs.append((((y * 8 + z) * 8 + x) * 4 + low, target))
    return pairs


def beside(parts):
    return jnp.concatenate([parts[i] for i in range(parts.shape[0])], axis=-1)


def products(own, far, pieces, x_lo):
    cores, places, tokens, hidden = own.shape
    rows = sum(piece.shape[0] for piece in pieces)

    def kernel(x_ref, own_ref, far_ref, *refs):
        piece_refs, out_ref = refs[:-1], refs[-1]
        here = x_ref[0]
        for slot, grads_ref in enumerate((own_ref, far_ref)):
            total = None
            for place in range(places):
                at = here if place == 0 else 1 - here
                for core in range(cores):
                    source = place * cores + core
                    columns = slice(source * hidden, (source + 1) * hidden)
                    weight = jnp.concatenate([ref[:, columns] for ref in piece_refs], axis=0)
                    term = lax.dot_general(
                        weight, grads_ref[core, at], (((1,), (1,)), ((), ())), preferred_element_type=jnp.float32
                    )
                    total = term if total is None else total + term
            out_ref[slot] = total.astype(jnp.bfloat16)

    in_vmem = pl.BlockSpec(memory_space=pltpu.VMEM)
    return pl.pallas_call(
        kernel,
        out_shape=jax.ShapeDtypeStruct((2, rows, tokens), jnp.bfloat16),
        in_specs=[pl.BlockSpec(memory_space=pltpu.SMEM)] + [in_vmem] * (2 + len(pieces)),
        out_specs=in_vmem,
        compiler_params=pltpu.CompilerParams(vmem_limit_bytes=12 * 1024 * 1024),
        cost_estimate=pl.CostEstimate(
            flops=4 * rows * tokens * cores * places * hidden, bytes_accessed=6000000, transcendentals=0
        ),
    )(x_lo.reshape(1).astype(jnp.int32), own, far, *pieces)


def on_device(pre_act, act_grad, up_weight, resid_grad, gram_parts, stripe_order, gram_prev):
    tokens, hidden = pre_act.shape
    feats = resid_grad.shape[1]

    hidden_grad = (act_grad.astype(jnp.float32) * gelu_slope(pre_act.astype(jnp.float32))).astype(jnp.bfloat16)
    far_grad = lax.ppermute(hidden_grad, "y_hi", SWAP)
    beside_grad = lax.ppermute(hidden_grad, "x_lo", SWAP)

    quarters = lax.all_to_all(up_weight.reshape(4, feats, hidden), QUAD, 0, 0, tiled=True)
    mine = beside(quarters)
    mine, hidden_grad = lax.optimization_barrier((mine, hidden_grad))
    ring = {0: mine}
    for step in (2, 6, 1, 7):
        ring[step] = from_z(mine, step)
    own = lax.all_gather(jnp.stack([hidden_grad, beside_grad]), "core", axis=0)
    own, parts, far_grad = lax.optimization_barrier((own, gram_parts[0], far_grad))
    far_beside = lax.ppermute(far_grad, "x_lo", SWAP)
    stripes = parts.reshape(lax.axis_size(("y_hi", "z")), -1, parts.shape[1])
    ordered = stripes[stripe_order[0]]

    mid = feats // 2
    halves = ring[2][:mid], ring[6][mid:]
    *first, far_beside, own, ordered = lax.optimization_barrier(
        (ring[1], ring[7], ring[2], ring[6], *halves, far_beside, own, ordered)
    )
    ring[1], ring[7], ring[2], ring[6], *halves = first
    far_pair = jnp.stack([far_grad, far_beside])
    upper, lower = from_z(halves[0], 2), from_z(halves[1], 6)
    ring[3] = from_z(ring[2], 1)
    ring[5] = from_z(ring[6], 7)
    far = lax.all_gather(far_pair, "core", axis=0)

    kept = lax.all_to_all(ordered, ("y_hi", "z"), 0, 0, tiled=True)
    upper, kept = lax.optimization_barrier((upper, kept))
    gram_stats = gram_prev + jnp.sum(kept.astype(jnp.float32), axis=0).reshape(gram_prev.shape)

    pieces = [ring[step] for step in ORDER[:-1]] + [upper, lower]
    blocks = products(own, far, pieces, lax.axis_index("x_lo")).reshape(-1, feats, tokens)
    arrived = lax.all_to_all(blocks, ("x_hi", "x_mid", "y_lo"), 0, 0, tiled=True)
    shared = jnp.sum(arrived.astype(jnp.float32), axis=0).astype(jnp.bfloat16)
    home = lax.ppermute(shared, WHERE, last_hop())
    input_grad = (home.astype(jnp.float32) + resid_grad.T.astype(jnp.float32)).astype(jnp.bfloat16).T
    return (input_grad, gram_stats)


def solution(mesh):
    axes = ("y_hi", "z", "x_hi", "x_mid", "x_lo", "y_lo", "core")
    fine = Mesh(mesh.devices.reshape(2, 8, 2, 2, 2, 4, 2), axes)
    replica, spread = axes[:2], axes[2:]
    return jax.shard_map(
        on_device,
        mesh=fine,
        in_specs=(
            P(replica, spread),
            P(replica, spread),
            P(replica, spread),
            P(replica, spread),
            P(replica, spread, None),
            P(spread, None),
            P(spread, replica, None, None),
        ),
        out_specs=(P(replica, spread), P(spread, replica, None, None)),
        check_vma=False,
    )
```

```python
import jax
import jax.numpy as jnp
from jax import lax
from jax.experimental import pallas as pl
from jax.experimental.pallas import tpu as pltpu
from jax.sharding import Mesh, PartitionSpec as P


def gelu_slope(values):
    normal_cdf = 0.5 * (1.0 + jax.scipy.special.erf(values * 0.7071067811865476))
    return normal_cdf + values * jnp.exp(-0.5 * values * values) * 0.3989422804014327


SWAP = [(0, 1), (1, 0)]
QUAD = ("x_lo", "core")
WHERE = ("y_hi", "z", "x_hi", "x_mid", "x_lo", "y_lo")
ORDER = (0, 1, 7, 2, 6, 3, 5, 4)


def from_z(value, step):
    return lax.ppermute(value, "z", [((i + step) % 8, i) for i in range(8)])


def last_hop():
    pairs = []
    for y in range(2):
        for z in range(8):
            for x in range(8):
                for low in range(4):
                    s, b, p = x >> 2, x & 1, ((x >> 1) & 1) * 4 + low
                    w = (z + ORDER[p]) % 8
                    target = (((y ^ s) * 8 + z) * 8 + y * 4 + (w >> 1)) * 4 + (w & 1) * 2 + b
                    pairs.append((((y * 8 + z) * 8 + x) * 4 + low, target))
    return pairs


def beside(parts):
    return jnp.concatenate([parts[i] for i in range(parts.shape[0])], axis=-1)


def products(own, far, pieces, feats, before=None):
    sources, tokens, hidden = own.shape
    rows = sum(piece.shape[0] for piece in pieces)
    done = 0 if before is None else before.shape[1]

    def kernel(*refs):
        own_ref, far_ref, out_ref = refs[0], refs[1], refs[-1]
        piece_refs = refs[2 : 2 + len(pieces)]
        for slot, grads_ref in enumerate((own_ref, far_ref)):
            total = None
            for source in range(sources):
                columns = slice(source * hidden, (source + 1) * hidden)
                weight = jnp.concatenate([ref[:, columns] for ref in piece_refs], axis=0)
                term = lax.dot_general(
                    weight, grads_ref[source], (((1,), (1,)), ((), ())), preferred_element_type=jnp.float32
                )
                total = term if total is None else total + term
            if before is not None:
                out_ref[slot, :done] = refs[2 + len(pieces)][slot]
            out_ref[slot, done:] = total.astype(jnp.bfloat16)

    operands = [own, far, *pieces] + ([] if before is None else [before])
    return pl.pallas_call(
        kernel,
        out_shape=jax.ShapeDtypeStruct((2, done + rows, tokens), jnp.bfloat16),
        in_specs=[pl.BlockSpec(memory_space=pltpu.VMEM)] * len(operands),
        out_specs=pl.BlockSpec(memory_space=pltpu.VMEM),
        compiler_params=pltpu.CompilerParams(vmem_limit_bytes=12 * 1024 * 1024),
        cost_estimate=pl.CostEstimate(
            flops=4 * rows * tokens * sources * hidden, bytes_accessed=6000000, transcendentals=0
        ),
    )(*operands)


def on_device(pre_act, act_grad, up_weight, resid_grad, gram_parts, stripe_order, gram_prev):
    tokens, hidden = pre_act.shape
    feats = resid_grad.shape[1]

    hidden_grad = (act_grad.astype(jnp.float32) * gelu_slope(pre_act.astype(jnp.float32))).astype(jnp.bfloat16)
    far_grad = lax.ppermute(hidden_grad, "y_hi", SWAP)

    quarters = lax.all_to_all(up_weight.reshape(4, feats, hidden), QUAD, 0, 0, tiled=True)
    mine = beside(quarters)
    mine, hidden_grad = lax.optimization_barrier((mine, hidden_grad))
    ring = {0: mine}
    for step in (2, 6, 1, 7):
        ring[step] = from_z(mine, step)
    own = lax.all_gather(hidden_grad, QUAD, axis=0)
    own, parts = lax.optimization_barrier((own, gram_parts[0]))
    stripes = parts.reshape(lax.axis_size(("y_hi", "z")), -1, parts.shape[1])
    ordered = stripes[stripe_order[0]]

    *first, far_grad, own, ordered = lax.optimization_barrier(
        (ring[1], ring[7], ring[2], ring[6], far_grad, own, ordered)
    )
    ring[1], ring[7], ring[2], ring[6] = first
    ring[3] = from_z(ring[2], 1)
    ring[5] = from_z(ring[6], 7)
    mid = feats // 2
    upper, lower = from_z(ring[2][:mid], 2), from_z(ring[6][mid:], 6)
    far = lax.all_gather(far_grad, QUAD, axis=0)
    kept = lax.all_to_all(ordered, ("y_hi", "z"), 0, 0, tiled=True)

    near = products(own, far, [ring[step] for step in ORDER[:5]], feats)
    upper, kept = lax.optimization_barrier((upper, kept))
    gram_stats = gram_prev + jnp.sum(kept.astype(jnp.float32), axis=0).reshape(gram_prev.shape)
    blocks = products(own, far, [ring[3], ring[5], upper, lower], feats, near)
    blocks = blocks.reshape(-1, feats, tokens)
    arrived = lax.all_to_all(blocks, ("x_hi", "x_mid", "y_lo"), 0, 0, tiled=True)
    shared = jnp.sum(arrived.astype(jnp.float32), axis=0).astype(jnp.bfloat16)
    home = lax.ppermute(shared, WHERE, last_hop())
    input_grad = (home.astype(jnp.float32) + resid_grad.T.astype(jnp.float32)).astype(jnp.bfloat16).T
    return (input_grad, gram_stats)


def solution(mesh):
    axes = ("y_hi", "z", "x_hi", "x_mid", "x_lo", "y_lo", "core")
    fine = Mesh(mesh.devices.reshape(2, 8, 2, 2, 2, 4, 2), axes)
    replica, spread = axes[:2], axes[2:]
    return jax.shard_map(
        on_device,
        mesh=fine,
        in_specs=(
            P(replica, spread),
            P(replica, spread),
            P(replica, spread),
            P(replica, spread),
            P(replica, spread, None),
            P(spread, None),
            P(spread, replica, None, None),
        ),
        out_specs=(P(replica, spread), P(spread, replica, None, None)),
        check_vma=False,
    )
```
